32 devices in a mesh: gx: 8 (over y, x, core), gy: 4 (over z).
Axes of the slice: x: 2, y: 2, z: 4, core: 2. Of those that a mesh axis runs over, the one named last changes fastest.
Arguments:
- orbitals: float32 [64, 32, 32, 128], P(None, 'gx', 'gy'), may hold values from -60 to 60, as said below
- potential: float32 [32, 32, 128], P('gx', 'gy'), may hold values from 0.2 to 2
Outputs:
- basis: float32 [64, 32, 32, 128], P(None, 'gx', 'gy')
- factor: float32 [64, 64], replicated
The draws below stay inside these ranges and needn't reach their ends.
Inputs may be any that keep to these rules, and one draw needn't show every extreme that they name: `orbitals`: Real-valued entries.
All inputs are finite; a program needn't handle non-finite values.
Results may differ from the reference program's by a relative error of at most 0.00011.
Values sent between devices are 32-bit elements; how exact they have to be, the bound alone decides.
A program may use at most 64 MiB of HBM per device.

```python
import math
import jax
import jax.numpy as jnp
from jax import lax

M = 64
NX = 32
NY = 32
NZ = 128


def draw_orbitals(key, part):
    key_base = jax.random.fold_in(jax.random.fold_in(key, 7), 0)
    spots = jnp.arange(NX, dtype=jnp.float32) / max(NX - 1, 1)
    profile = (1.0 + 2.0 * spots)[None, :, None, None]
    base = jax.random.truncated_normal(key_base, -4.0, 4.0, (M, NX, NY, NZ), jnp.float32)
    return base * profile


def steps_of(rng, extent, pieces, smallest, high):
    factor_of = 1.0
    for position, parts in pieces:
        steps = jax.random.uniform(jax.random.fold_in(jax.random.fold_in(rng, 6), position), (parts,), jnp.float32, smallest / len(pieces), high / len(pieces))
        factor_of = factor_of * jnp.repeat(jnp.exp(steps), extent[position] // parts).reshape((-1,) + (1,) * (len(extent) - 1 - position))
    return factor_of


def setup_inputs(seed: int = 0) -> dict:
    key_list = jax.random.split(jax.random.key(seed), 3)
    return {
        "orbitals": draw_orbitals(jax.random.fold_in(key_list[2], 71), 0),
        "potential": jnp.clip(jnp.exp(math.log(2.0) - 2.3025851 * jax.random.uniform(key_list[1], (NX, NY, NZ), jnp.float32) ** steps_of(key_list[1], (NX, NY, NZ), ((0, 8), (1, 4)), -0.2, 0.2)), 0.2, 2.0),
    }


def laplace_roll(field):
    total = jnp.zeros_like(field)
    for axis_num in range(3):
        total = total - 2.5 * field
        total = total + 4.0 / 3.0 * (jnp.roll(field, 1, axis_num) + jnp.roll(field, -1, axis_num))
        total = total - 1.0 / 12.0 * (jnp.roll(field, 2, axis_num) + jnp.roll(field, -2, axis_num))
    return total

def filter_one(field, potential):
    first = (-0.5 * laplace_roll(field) + potential * field - 5.5 * field) / 4.5
    applied = -0.5 * laplace_roll(first) + potential * first
    return 2.0 * (applied - 5.5 * first) / 4.5 - field

def reference(orbitals, potential):
    filtered = lax.map(lambda one: filter_one(one, potential), orbitals)
    cells = NX * NY * NZ
    flat = filtered.reshape(M, cells)
    gram = jnp.dot(flat.astype(jnp.float32), flat.T.astype(jnp.float32), precision=lax.Precision.HIGHEST, preferred_element_type=jnp.float32) / cells
    factor = lax.linalg.cholesky(gram).T
    solved = lax.linalg.triangular_solve(factor, flat, left_side=True, lower=False, transpose_a=True)
    basis = (solved * jnp.sqrt(jnp.float32(cells))).reshape(M, NX, NY, NZ)
    return (basis, factor)
```

```python
import functools

import jax
import jax.numpy as jnp
from jax import lax
from jax.experimental import pallas as pl
from jax.experimental.pallas import tpu as pltpu
from jax.sharding import PartitionSpec as P

MESH = pl.DeviceIdType.MESH
CHUNKS = 4


def pick(row, bound, a, b):
    return jnp.where(row < bound, a, b)


def pack_low(tiles, row):
    out = tiles[3]
    out = pltpu.roll(out, 6, 0)
    out = pick(row, 6, pltpu.roll(tiles[2], 4, 0), out)
    out = pick(row, 4, pltpu.roll(tiles[1], 2, 0), out)
    return pick(row, 2, tiles[0], out)


def pack_high(tiles, row):
    out = tiles[3]
    out = pick(row, 6, pltpu.roll(tiles[2], 6, 0), out)
    out = pick(row, 4, pltpu.roll(tiles[1], 4, 0), out)
    return pick(row, 2, pltpu.roll(tiles[0], 2, 0), out)


def unroll_low(packed, layer):
    return packed if layer == 0 else pltpu.roll(packed, 8 - 2 * layer, 0)


def unroll_high(packed, layer):
    return packed if layer == 3 else pltpu.roll(packed, 6 - 2 * layer, 0)


def stencil(core, below, above, ylow, yhigh, diag, row):
    near, far = -2.0 / 3.0 / 4.5, 1.0 / 24.0 / 4.5
    layers = below + core + above
    outs = []
    for x in range(4):
        c = core[x]
        top = unroll_low(ylow, x)
        bottom = unroll_high(yhigh, x)
        s1 = layers[x + 1] + layers[x + 3]
        s2 = layers[x] + layers[x + 4]
        s1 = s1 + pltpu.roll(jnp.where(row < 1, top, c), 7, 0)
        s2 = s2 + pltpu.roll(jnp.where(row < 2, top, c), 6, 0)
        s1 = s1 + pltpu.roll(jnp.where(row < 7, c, bottom), 1, 0)
        s2 = s2 + pltpu.roll(jnp.where(row < 6, c, bottom), 2, 0)
        s1 = s1 + pltpu.roll(c, 1, 1) + pltpu.roll(c, 127, 1)
        s2 = s2 + pltpu.roll(c, 2, 1) + pltpu.roll(c, 126, 1)
        outs.append(diag[x] * c + near * s1 + far * s2)
    return outs


def split3(value):
    high = value.astype(jnp.bfloat16)
    rest = value - high.astype(jnp.float32)
    middle = rest.astype(jnp.bfloat16)
    low = (rest - middle.astype(jnp.float32)).astype(jnp.bfloat16)
    return high, middle, low


def filter_kernel(
    nx, ny, orb, pot, flat_out, gram_out,
    first, filt, xlo, xhi, ylo, yhi, pklo, pkhi, gsend, grs, gsum, gex,
    xs, xr, ys, yr, rss, rsr, exs, exr, ags, agr,
):
    gx, gy = lax.axis_index("gx"), lax.axis_index("gy")
    left, right = lax.rem(gx + nx - 1, nx), lax.rem(gx + 1, nx)
    down, up = lax.rem(gy + ny - 1, ny), lax.rem(gy + 1, ny)
    width = orb.shape[0]
    size = width // CHUNKS
    row = lax.broadcasted_iota(jnp.int32, (8, 128), 0)

    barrier = pltpu.get_barrier_semaphore()
    for k in range(1, nx):
        pl.semaphore_signal(barrier, inc=1, device_id=(lax.rem(gx + k, nx), gy), device_id_type=MESH)
    for k in range(1, ny):
        pl.semaphore_signal(barrier, inc=1, device_id=(gx, lax.rem(gy + k, ny)), device_id_type=MESH)

    diag = [(pot[x] - 1.75) / 4.5 for x in range(4)]

    def pack(o, tiles, phase):
        pklo[phase, o] = pack_low(tiles, row)
        pkhi[phase, o] = pack_high(tiles, row)

    def copies(phase, chunk, source):
        span = pl.ds(chunk * size, size)
        n = (phase, chunk)
        make = pltpu.make_async_remote_copy
        return [
            make(source.at[span, 0:2], xhi.at[phase, span], xs.at[*n, 0], xr.at[*n, 0],
                 device_id=(left, gy), device_id_type=MESH),
            make(source.at[span, 2:4], xlo.at[phase, span], xs.at[*n, 1], xr.at[*n, 1],
                 device_id=(right, gy), device_id_type=MESH),
            make(pklo.at[phase, span], ylo.at[phase, span], ys.at[*n, 0], yr.at[*n, 0],
                 device_id=(gx, down), device_id_type=MESH),
            make(pkhi.at[phase, span], yhi.at[phase, span], ys.at[*n, 1], yr.at[*n, 1],
                 device_id=(gx, up), device_id_type=MESH),
        ]

    @pl.loop(0, width, unroll=4)
    def _(o):
        pack(o, [orb[o, x] for x in range(4)], 0)

    pl.semaphore_wait(barrier, nx + ny - 2)
    flights = []
    for chunk in range(CHUNKS):
        for copy in copies(0, chunk, orb):
            copy.start()
            flights.append(copy)

    for phase in range(2):
        source = (orb, first)[phase]
        for chunk in range(CHUNKS):
            for copy in copies(phase, chunk, source):
                copy.wait_recv()

            @pl.loop(chunk * size, (chunk + 1) * size, unroll=2)
            def _(o):
                tiles = stencil(
                    [source[o, x] for x in range(4)],
                    [xlo[phase, o, x] for x in range(2)],
                    [xhi[phase, o, x] for x in range(2)],
                    ylo[phase, o], yhi[phase, o], diag, row,
                )
                if phase == 0:
                    for x in range(4):
                        first[o, x] = tiles[x]
                    pack(o, tiles, 1)
                else:
                    for x in range(4):
                        filt[pl.ds(pl.multiple_of(o * 32 + 8 * x, 8), 8), :] = 2.0 * tiles[x] - orb[o, x]

            if phase == 0:
                for copy in copies(1, chunk, first):
                    copy.start()
                    flights.append(copy)

    for r in range(32):
        flat_out[:, r * 128:(r + 1) * 128] = filt[pl.ds(r, width, stride=32), :]
    gram = jnp.zeros((3 * width, 3 * width), jnp.float32)
    for step in range(8):
        parts = jnp.concatenate(split3(flat_out[:, step * 512:(step + 1) * 512]), axis=0)
        gram = gram + lax.dot_general(
            parts, parts, (((1,), (1,)), ((), ())), preferred_element_type=jnp.float32
        )
    total = jnp.zeros((width, 3 * width), jnp.float32)
    for a in (2, 1, 0):
        total = total + gram[a * width:(a + 1) * width]
    total = total[:, 2 * width:] + total[:, width:2 * width] + total[:, :width]
    cells = 4096 * nx * ny
    total = jnp.concatenate([total, jnp.zeros_like(total)], axis=1) / cells
    rows = width // nx
    for i in range(nx):
        gsend[i] = total[i * rows:(i + 1) * rows]

    step1 = []
    for k in range(1, nx):
        to = lax.rem(gx + k, nx)
        copy = pltpu.make_async_remote_copy(
            gsend.at[to], grs.at[k], rss.at[k], rsr.at[k], device_id=(to, gy), device_id_type=MESH)
        copy.start()
        step1.append(copy)
    mine = gsend[gx]
    for k in range(1, nx):
        step1[k - 1].wait_recv()
        mine = mine + grs[k]
    gex[gy] = mine
    step2 = []
    for k in range(1, ny):
        copy = pltpu.make_async_remote_copy(
            gex.at[gy], gex.at[gy], exs.at[k], exr.at[k],
            device_id=(gx, lax.rem(gy + k, ny)), device_id_type=MESH)
        copy.start()
        step2.append(copy)
    for copy in step2:
        copy.wait_recv()
    mine = gex[0]
    for j in range(1, ny):
        mine = mine + gex[j]
    gsum[gx] = mine
    step3 = []
    for k in range(1, nx):
        copy = pltpu.make_async_remote_copy(
            gsum.at[gx], gsum.at[gx], ags.at[k], agr.at[k],
            device_id=(lax.rem(gx + k, nx), gy), device_id_type=MESH)
        copy.start()
        step3.append(copy)
    for copy in step3:
        copy.wait_recv()
    for i in range(nx):
        gram_out[i * rows:(i + 1) * rows, :] = gsum[i]
    for copy in flights + step1 + step2 + step3:
        copy.wait_send()


def solve_kernel(cells, flat, gram, basis, factor):
    width = flat.shape[0]
    groups = width // 8
    lane = lax.broadcasted_iota(jnp.int32, (8, 128), 1)
    row = lax.broadcasted_iota(jnp.int32, (8, 128), 0)
    work = []
    for t in range(groups):
        unit = jnp.where(lane == row + 8 * t + width, 1.0, 0.0)
        work.append(jnp.where(lane < width, gram[8 * t:8 * t + 8, :], unit))
    for k in range(width):
        t0, r = divmod(k, 8)
        factors = [
            jnp.broadcast_to(work[t][:, k:k + 1], (8, 128)) if t >= t0 else None
            for t in range(groups)
        ]
        pivot = jnp.broadcast_to(factors[t0][r:r + 1], (8, 128))
        line = jnp.broadcast_to(work[t0][r:r + 1], (8, 128)) / pivot
        for t in range(t0, groups):
            less = factors[t] * line
            if t == t0:
                less = jnp.where(row > r, less, 0.0)
            work[t] = work[t] - less
    upper = []
    for t in range(groups):
        pivots = jnp.sum(jnp.where(lane == row + 8 * t, work[t], 0.0), axis=1, keepdims=True)
        work[t] = work[t] * (1.0 / jnp.sqrt(pivots))
        upper.append(jnp.where(lane < row + 8 * t, 0.0, work[t]))
    whole = jnp.concatenate(upper, axis=0)
    factor[...] = whole[:, :width]
    inverse = jnp.concatenate(work, axis=0)[:, width:] * (float(cells) ** 0.5)
    a, b, c = split3(inverse)
    lhs = jnp.concatenate([a, b, a, c, b, a], axis=1)
    for step in range(8):
        y1, y2, y3 = split3(flat[:, step * 512:(step + 1) * 512])
        rhs = jnp.concatenate([y1, y1, y2, y1, y2, y3], axis=0)
        out = jnp.dot(lhs, rhs, preferred_element_type=jnp.float32)
        for i in range(4):
            basis[pl.ds(step * 4 + i, width, stride=32), :] = out[:, i * 128:(i + 1) * 128]


def shards(mesh, orbitals, potential):
    nx, ny = mesh.shape["gx"], mesh.shape["gy"]
    width = orbitals.shape[0]
    local = orbitals.shape[1] * orbitals.shape[2] * orbitals.shape[3]
    rows = width // nx
    f32 = jnp.float32
    vmem = pl.BlockSpec(memory_space=pltpu.VMEM)
    dma = pltpu.SemaphoreType.DMA
    flat, gram = pl.pallas_call(
        functools.partial(filter_kernel, nx, ny),
        out_shape=[
            jax.ShapeDtypeStruct((width, local), f32),
            jax.ShapeDtypeStruct((width, 128), f32),
        ],
        in_specs=[vmem, vmem],
        out_specs=[vmem, vmem],
        scratch_shapes=[
            pltpu.VMEM(orbitals.shape, f32),
            pltpu.VMEM((width * 32, 128), f32),
            pltpu.VMEM((2, width, 2, 8, 128), f32),
            pltpu.VMEM((2, width, 2, 8, 128), f32),
            pltpu.VMEM((2, width, 8, 128), f32),
            pltpu.VMEM((2, width, 8, 128), f32),
            pltpu.VMEM((2, width, 8, 128), f32),
            pltpu.VMEM((2, width, 8, 128), f32),
            pltpu.VMEM((nx, rows, 128), f32),
            pltpu.VMEM((nx, rows, 128), f32),
            pltpu.VMEM((nx, rows, 128), f32),
            pltpu.VMEM((ny, rows, 128), f32),
            dma((2, CHUNKS, 2)), dma((2, CHUNKS, 2)), dma((2, CHUNKS, 2)), dma((2, CHUNKS, 2)),
            dma((nx,)), dma((nx,)), dma((ny,)), dma((ny,)), dma((nx,)), dma((nx,)),
        ],
        compiler_params=pltpu.CompilerParams(
            collective_id=0, has_side_effects=True, vmem_limit_bytes=32 << 20
        ),
        name="filter",
    )(orbitals, potential)
    basis, factor = pl.pallas_call(
        functools.partial(solve_kernel, local * nx * ny),
        out_shape=[
            jax.ShapeDtypeStruct((width * 32, 128), f32),
            jax.ShapeDtypeStruct((width, width), f32),
        ],
        in_specs=[vmem, vmem],
        out_specs=[vmem, vmem],
        compiler_params=pltpu.CompilerParams(vmem_limit_bytes=32 << 20),
        name="solve",
    )(flat, gram)
    return basis.reshape(orbitals.shape), factor


def solution(mesh):
    return jax.shard_map(
        functools.partial(shards, mesh),
        mesh=mesh,
        in_specs=(P(None, "gx", "gy", None), P("gx", "gy", None)),
        out_specs=(P(None, "gx", "gy", None), P()),
        check_vma=False,
    )
```

```python
import functools

import jax
import jax.numpy as jnp
from jax import lax
from jax.experimental import pallas as pl
from jax.experimental.pallas import tpu as pltpu
from jax.sharding import PartitionSpec as P

MESH = pl.DeviceIdType.MESH
CHUNKS = 4
LIMIT = 52 << 20


def pick(row, bound, a, b):
    return jnp.where(row < bound, a, b)


def pack_low(tiles, row):
    out = tiles[3]
    out = pltpu.roll(out, 6, 0)
    out = pick(row, 6, pltpu.roll(tiles[2], 4, 0), out)
    out = pick(row, 4, pltpu.roll(tiles[1], 2, 0), out)
    return pick(row, 2, tiles[0], out)


def pack_high(tiles, row):
    out = tiles[3]
    out = pick(row, 6, pltpu.roll(tiles[2], 6, 0), out)
    out = pick(row, 4, pltpu.roll(tiles[1], 4, 0), out)
    return pick(row, 2, pltpu.roll(tiles[0], 2, 0), out)


def unroll_low(packed, layer):
    return packed if layer == 0 else pltpu.roll(packed, 8 - 2 * layer, 0)


def unroll_high(packed, layer):
    return packed if layer == 3 else pltpu.roll(packed, 6 - 2 * layer, 0)


def stencil(core, below, above, ylow, yhigh, diag, row):
    near, far = -2.0 / 3.0 / 4.5, 1.0 / 24.0 / 4.5
    layers = below + core + above
    outs = []
    for x in range(4):
        c = core[x]
        top = unroll_low(ylow, x)
        bottom = unroll_high(yhigh, x)
        s1 = layers[x + 1] + layers[x + 3]
        s2 = layers[x] + layers[x + 4]
        s1 = s1 + pltpu.roll(jnp.where(row < 1, top, c), 7, 0)
        s2 = s2 + pltpu.roll(jnp.where(row < 2, top, c), 6, 0)
        s1 = s1 + pltpu.roll(jnp.where(row < 7, c, bottom), 1, 0)
        s2 = s2 + pltpu.roll(jnp.where(row < 6, c, bottom), 2, 0)
        s1 = s1 + pltpu.roll(c, 1, 1) + pltpu.roll(c, 127, 1)
        s2 = s2 + pltpu.roll(c, 2, 1) + pltpu.roll(c, 126, 1)
        outs.append(diag[x] * c + near * s1 + far * s2)
    return outs


def split3(value):
    high = value.astype(jnp.bfloat16)
    rest = value - high.astype(jnp.float32)
    middle = rest.astype(jnp.bfloat16)
    low = (rest - middle.astype(jnp.float32)).astype(jnp.bfloat16)
    return high, middle, low


def filter_kernel(
    nx, ny, orb_hbm, pot_hbm, flat_out, gram_out,
    orb, pot, flat, first, filt, xlo, xhi, ylo, yhi, pklo, pkhi, gsend, grs, gsum, gex,
    lds, svs, xs, xr, ys, yr, rss, rsr, exs, exr, ags, agr,
):
    gx, gy = lax.axis_index("gx"), lax.axis_index("gy")
    left, right = lax.rem(gx + nx - 1, nx), lax.rem(gx + 1, nx)
    down, up = lax.rem(gy + ny - 1, ny), lax.rem(gy + 1, ny)
    width = orb.shape[0]
    size = width // CHUNKS
    loads = [
        pltpu.make_async_copy(
            orb_hbm.at[c * size:(c + 1) * size], orb.at[c * size:(c + 1) * size], lds.at[c])
        for c in range(CHUNKS)
    ] + [pltpu.make_async_copy(pot_hbm, pot, lds.at[CHUNKS])]
    for load in loads:
        load.start()
    row = lax.broadcasted_iota(jnp.int32, (8, 128), 0)

    barrier = pltpu.get_barrier_semaphore()
    for k in range(1, nx):
        pl.semaphore_signal(barrier, inc=1, device_id=(lax.rem(gx + k, nx), gy), device_id_type=MESH)
    for k in range(1, ny):
        pl.semaphore_signal(barrier, inc=1, device_id=(gx, lax.rem(gy + k, ny)), device_id_type=MESH)


    def pack(o, tiles, phase):
        pklo[phase, o] = pack_low(tiles, row)
        pkhi[phase, o] = pack_high(tiles, row)

    def copies(phase, chunk, source):
        span = pl.ds(chunk * size, size)
        n = (phase, chunk)
        make = pltpu.make_async_remote_copy
        return [
            make(source.at[span, 0:2], xhi.at[phase, span], xs.at[*n, 0], xr.at[*n, 0],
                 device_id=(left, gy), device_id_type=MESH),
            make(source.at[span, 2:4], xlo.at[phase, span], xs.at[*n, 1], xr.at[*n, 1],
                 device_id=(right, gy), device_id_type=MESH),
            make(pklo.at[phase, span], ylo.at[phase, span], ys.at[*n, 0], yr.at[*n, 0],
                 device_id=(gx, down), device_id_type=MESH),
            make(pkhi.at[phase, span], yhi.at[phase, span], ys.at[*n, 1], yr.at[*n, 1],
                 device_id=(gx, up), device_id_type=MESH),
        ]

    flights, saves = [], []
    for chunk in range(CHUNKS):
        loads[chunk].wait()

        @pl.loop(chunk * size, (chunk + 1) * size, unroll=4)
        def _(o):
            pack(o, [orb[o, x] for x in range(4)], 0)

        if chunk == 0:
            pl.semaphore_wait(barrier, nx + ny - 2)
        for copy in copies(0, chunk, orb):
            copy.start()
            flights.append(copy)
    loads[CHUNKS].wait()
    diag = [(pot[x] - 1.75) / 4.5 for x in range(4)]

    for phase in range(2):
        source = (orb, first)[phase]
        for chunk in range(CHUNKS):
            for copy in copies(phase, chunk, source):
                copy.wait_recv()

            @pl.loop(chunk * size, (chunk + 1) * size, unroll=2)
            def _(o):
                tiles = stencil(
                    [source[o, x] for x in range(4)],
                    [xlo[phase, o, x] for x in range(2)],
                    [xhi[phase, o, x] for x in range(2)],
                    ylo[phase, o], yhi[phase, o], diag, row,
                )
                if phase == 0:
                    for x in range(4):
                        first[o, x] = tiles[x]
                    pack(o, tiles, 1)
                else:
                    for x in range(4):
                        filt[pl.ds(pl.multiple_of(o * 32 + 8 * x, 8), 8), :] = 2.0 * tiles[x] - orb[o, x]

            if phase == 0:
                for copy in copies(1, chunk, first):
                    copy.start()
                    flights.append(copy)
            else:
                span = slice(chunk * size, (chunk + 1) * size)
                for r in range(32):
                    flat[span, r * 128:(r + 1) * 128] = filt[
                        pl.ds(chunk * size * 32 + r, size, stride=32), :]
                save = pltpu.make_async_copy(flat.at[span], flat_out.at[span], svs.at[chunk])
                save.start()
                saves.append(save)

    gram = jnp.zeros((3 * width, 3 * width), jnp.float32)
    for step in range(8):
        parts = jnp.concatenate(split3(flat[:, step * 512:(step + 1) * 512]), axis=0)
        gram = gram + lax.dot_general(
            parts, parts, (((1,), (1,)), ((), ())), preferred_element_type=jnp.float32
        )
    total = jnp.zeros((width, 3 * width), jnp.float32)
    for a in (2, 1, 0):
        total = total + gram[a * width:(a + 1) * width]
    total = total[:, 2 * width:] + total[:, width:2 * width] + total[:, :width]
    cells = 4096 * nx * ny
    total = jnp.concatenate([total, jnp.zeros_like(total)], axis=1) / cells
    rows = width // nx
    for i in range(nx):
        gsend[i] = total[i * rows:(i + 1) * rows]

    step1 = []
    for k in range(1, nx):
        to = lax.rem(gx + k, nx)
        copy = pltpu.make_async_remote_copy(
            gsend.at[to], grs.at[k], rss.at[k], rsr.at[k], device_id=(to, gy), device_id_type=MESH)
        copy.start()
        step1.append(copy)
    mine = gsend[gx]
    for k in range(1, nx):
        step1[k - 1].wait_recv()
        mine = mine + grs[k]
    gex[gy] = mine
    step2 = []
    for k in range(1, ny):
        copy = pltpu.make_async_remote_copy(
            gex.at[gy], gex.at[gy], exs.at[k], exr.at[k],
            device_id=(gx, lax.rem(gy + k, ny)), device_id_type=MESH)
        copy.start()
        step2.append(copy)
    for copy in step2:
        copy.wait_recv()
    mine = gex[0]
    for j in range(1, ny):
        mine = mine + gex[j]
    gsum[gx] = mine
    step3 = []
    for k in range(1, nx):
        copy = pltpu.make_async_remote_copy(
            gsum.at[gx], gsum.at[gx], ags.at[k], agr.at[k],
            device_id=(lax.rem(gx + k, nx), gy), device_id_type=MESH)
        copy.start()
        step3.append(copy)
    for copy in step3:
        copy.wait_recv()
    for i in range(nx):
        gram_out[i * rows:(i + 1) * rows, :] = gsum[i]
    for copy in flights + step1 + step2 + step3:
        copy.wait_send()
    for save in saves:
        save.wait()


def solve_kernel(cells, flat_hbm, gram, basis, factor, flat, held, sems):
    load = pltpu.make_async_copy(flat_hbm, flat, sems.at[4])
    load.start()
    width = flat.shape[0]
    groups = width // 8
    lane = lax.broadcasted_iota(jnp.int32, (8, 128), 1)
    row = lax.broadcasted_iota(jnp.int32, (8, 128), 0)
    work = []
    for t in range(groups):
        unit = jnp.where(lane == row + 8 * t + width, 1.0, 0.0)
        work.append(jnp.where(lane < width, gram[8 * t:8 * t + 8, :], unit))
    for p in range(groups):
        spread = [
            [jnp.broadcast_to(work[t][:, 8 * p + k:8 * p + k + 1], (8, 128)) for k in range(8)]
            if t >= p else None
            for t in range(groups)
        ]
        block = [
            [jnp.broadcast_to(spread[p][j][i:i + 1], (8, 128)) for j in range(i + 1)]
            for i in range(8)
        ]
        lines = [jnp.broadcast_to(work[p][k:k + 1], (8, 128)) for k in range(8)]
        roots = []
        for k in range(8):
            inv = 1.0 / block[k][k]
            roots.append(1.0 / jnp.sqrt(block[k][k]))
            scale = [block[i][k] * inv if i > k else None for i in range(8)]
            for i in range(k + 1, 8):
                for j in range(k + 1, i + 1):
                    block[i][j] = block[i][j] - scale[i] * block[j][k]
                lines[i] = lines[i] - scale[i] * lines[k]
            for t in range(p + 1, groups):
                column = spread[t][k]
                for j in range(k + 1, 8):
                    spread[t][j] = spread[t][j] - scale[j] * column
                work[t] = work[t] - (column * inv) * lines[k]
        tile = lines[7] * roots[7]
        for k in range(6, -1, -1):
            tile = jnp.where(row == k, lines[k] * roots[k], tile)
        work[p] = tile
    upper = []
    for t in range(groups):
        upper.append(jnp.where(lane < row + 8 * t, 0.0, work[t]))
    whole = jnp.concatenate(upper, axis=0)
    factor[...] = whole[:, :width]
    inverse = jnp.concatenate(work, axis=0)[:, width:] * (float(cells) ** 0.5)
    a, b, c = split3(inverse)
    lhs = jnp.concatenate([a, b, a, c, b, a], axis=1)
    lines = held.reshape(width * 32, 128)
    stores = []
    load.wait()
    for x in range(4):
        for part in (2 * x, 2 * x + 1):
            y1, y2, y3 = split3(flat[:, part * 512:(part + 1) * 512])
            rhs = jnp.concatenate([y1, y1, y2, y1, y2, y3], axis=0)
            out = jnp.dot(lhs, rhs, preferred_element_type=jnp.float32)
            for i in range(4):
                lines[pl.ds(part * 4 + i, width, stride=32), :] = out[:, i * 128:(i + 1) * 128]
        store = pltpu.make_async_copy(held.at[:, 8 * x:8 * x + 8], basis.at[:, x], sems.at[x])
        store.start()
        stores.append(store)
    for store in stores:
        store.wait()


def shards(mesh, orbitals, potential):
    nx, ny = mesh.shape["gx"], mesh.shape["gy"]
    width = orbitals.shape[0]
    local = orbitals.shape[1] * orbitals.shape[2] * orbitals.shape[3]
    rows = width // nx
    f32 = jnp.float32
    vmem = pl.BlockSpec(memory_space=pltpu.VMEM)
    hbm = pl.BlockSpec(memory_space=pltpu.HBM)
    dma = pltpu.SemaphoreType.DMA
    flat, gram = pl.pallas_call(
        functools.partial(filter_kernel, nx, ny),
        out_shape=[
            jax.ShapeDtypeStruct((width, local), f32),
            jax.ShapeDtypeStruct((width, 128), f32),
        ],
        in_specs=[hbm, hbm],
        out_specs=[hbm, vmem],
        scratch_shapes=[
            pltpu.VMEM(orbitals.shape, f32),
            pltpu.VMEM(potential.shape, f32),
            pltpu.VMEM((width, local), f32),
            pltpu.VMEM(orbitals.shape, f32),
            pltpu.VMEM((width * 32, 128), f32),
            pltpu.VMEM((2, width, 2, 8, 128), f32),
            pltpu.VMEM((2, width, 2, 8, 128), f32),
            pltpu.VMEM((2, width, 8, 128), f32),
            pltpu.VMEM((2, width, 8, 128), f32),
            pltpu.VMEM((2, width, 8, 128), f32),
            pltpu.VMEM((2, width, 8, 128), f32),
            pltpu.VMEM((nx, rows, 128), f32),
            pltpu.VMEM((nx, rows, 128), f32),
            pltpu.VMEM((nx, rows, 128), f32),
            pltpu.VMEM((ny, rows, 128), f32),
            dma((CHUNKS + 1,)), dma((CHUNKS,)),
            dma((2, CHUNKS, 2)), dma((2, CHUNKS, 2)), dma((2, CHUNKS, 2)), dma((2, CHUNKS, 2)),
            dma((nx,)), dma((nx,)), dma((ny,)), dma((ny,)), dma((nx,)), dma((nx,)),
        ],
        compiler_params=pltpu.CompilerParams(
            collective_id=0, has_side_effects=True, vmem_limit_bytes=LIMIT
        ),
        name="filter",
    )(orbitals, potential)
    basis, factor = pl.pallas_call(
        functools.partial(solve_kernel, local * nx * ny),
        out_shape=[
            jax.ShapeDtypeStruct(orbitals.shape, f32),
            jax.ShapeDtypeStruct((width, width), f32),
        ],
        in_specs=[hbm, vmem],
        out_specs=[hbm, vmem],
        scratch_shapes=[pltpu.VMEM((width, local), f32), pltpu.VMEM((width, 32, 128), f32), dma((5,))],
        compiler_params=pltpu.CompilerParams(vmem_limit_bytes=16 << 20),
        name="solve",
    )(flat, gram)
    return basis, factor


def solution(mesh):
    return jax.shard_map(
        functools.partial(shards, mesh),
        mesh=mesh,
        in_specs=(P(None, "gx", "gy", None), P("gx", "gy", None)),
        out_specs=(P(None, "gx", "gy", None), P()),
        check_vma=False,
    )
```

```python
import functools

import jax
import jax.numpy as jnp
from jax import lax
from jax.experimental import pallas as pl
from jax.experimental.pallas import tpu as pltpu
from jax.sharding import PartitionSpec as P

MESH = pl.DeviceIdType.MESH
CHUNKS = 4
LIMIT = 52 << 20


def pick(row, bound, a, b):
    return jnp.where(row < bound, a, b)


def pack_low(tiles, row):
    out = tiles[3]
    out = pltpu.roll(out, 6, 0)
    out = pick(row, 6, pltpu.roll(tiles[2], 4, 0), out)
    out = pick(row, 4, pltpu.roll(tiles[1], 2, 0), out)
    return pick(row, 2, tiles[0], out)


def pack_high(tiles, row):
    out = tiles[3]
    out = pick(row, 6, pltpu.roll(tiles[2], 6, 0), out)
    out = pick(row, 4, pltpu.roll(tiles[1], 4, 0), out)
    return pick(row, 2, pltpu.roll(tiles[0], 2, 0), out)


def unroll_low(packed, layer):
    return packed if layer == 0 else pltpu.roll(packed, 8 - 2 * layer, 0)


def unroll_high(packed, layer):
    return packed if layer == 3 else pltpu.roll(packed, 6 - 2 * layer, 0)


def stencil(core, below, above, ylow, yhigh, diag, row):
    near, far = -2.0 / 3.0 / 4.5, 1.0 / 24.0 / 4.5
    layers = below + core + above
    outs = []
    for x in range(4):
        c = core[x]
        top = unroll_low(ylow, x)
        bottom = unroll_high(yhigh, x)
        s1 = layers[x + 1] + layers[x + 3]
        s2 = layers[x] + layers[x + 4]
        s1 = s1 + pltpu.roll(jnp.where(row < 1, top, c), 7, 0)
        s2 = s2 + pltpu.roll(jnp.where(row < 2, top, c), 6, 0)
        s1 = s1 + pltpu.roll(jnp.where(row < 7, c, bottom), 1, 0)
        s2 = s2 + pltpu.roll(jnp.where(row < 6, c, bottom), 2, 0)
        s1 = s1 + pltpu.roll(c, 1, 1) + pltpu.roll(c, 127, 1)
        s2 = s2 + pltpu.roll(c, 2, 1) + pltpu.roll(c, 126, 1)
        outs.append(diag[x] * c + near * s1 + far * s2)
    return outs


def split3(value):
    high = value.astype(jnp.bfloat16)
    rest = value - high.astype(jnp.float32)
    middle = rest.astype(jnp.bfloat16)
    low = (rest - middle.astype(jnp.float32)).astype(jnp.bfloat16)
    return high, middle, low


def filter_kernel(
    nx, ny, orb_hbm, pot_hbm, flat_out, gram_out,
    orb, pot, flat, first, filt, xlo, xhi, ylo, yhi, pklo, pkhi, gsend, grs, gsum, gex,
    lds, svs, xs, xr, ys, yr, rss, rsr, exs, exr, ags, agr,
):
    gx, gy = lax.axis_index("gx"), lax.axis_index("gy")
    left, right = lax.rem(gx + nx - 1, nx), lax.rem(gx + 1, nx)
    down, up = lax.rem(gy + ny - 1, ny), lax.rem(gy + 1, ny)
    width = orb.shape[0]
    size = width // CHUNKS
    loads = [
        pltpu.make_async_copy(
            orb_hbm.at[c * size:(c + 1) * size], orb.at[c * size:(c + 1) * size], lds.at[c])
        for c in range(CHUNKS)
    ] + [pltpu.make_async_copy(pot_hbm, pot, lds.at[CHUNKS])]
    for load in loads:
        load.start()
    row = lax.broadcasted_iota(jnp.int32, (8, 128), 0)

    barrier = pltpu.get_barrier_semaphore()
    for k in range(1, nx):
        pl.semaphore_signal(barrier, inc=1, device_id=(lax.rem(gx + k, nx), gy), device_id_type=MESH)
    for k in range(1, ny):
        pl.semaphore_signal(barrier, inc=1, device_id=(gx, lax.rem(gy + k, ny)), device_id_type=MESH)


    def pack(o, tiles, phase):
        pklo[phase, o] = pack_low(tiles, row)
        pkhi[phase, o] = pack_high(tiles, row)

    def copies(phase, chunk, source):
        span = pl.ds(chunk * size, size)
        n = (phase, chunk)
        make = pltpu.make_async_remote_copy
        return [
            make(source.at[span, 0:2], xhi.at[phase, span], xs.at[*n, 0], xr.at[*n, 0],
                 device_id=(left, gy), device_id_type=MESH),
            make(source.at[span, 2:4], xlo.at[phase, span], xs.at[*n, 1], xr.at[*n, 1],
                 device_id=(right, gy), device_id_type=MESH),
            make(pklo.at[phase, span], ylo.at[phase, span], ys.at[*n, 0], yr.at[*n, 0],
                 device_id=(gx, down), device_id_type=MESH),
            make(pkhi.at[phase, span], yhi.at[phase, span], ys.at[*n, 1], yr.at[*n, 1],
                 device_id=(gx, up), device_id_type=MESH),
        ]

    flights, saves = [], []
    for chunk in range(CHUNKS):
        loads[chunk].wait()

        @pl.loop(chunk * size, (chunk + 1) * size, unroll=4)
        def _(o):
            pack(o, [orb[o, x] for x in range(4)], 0)

        if chunk == 0:
            pl.semaphore_wait(barrier, nx + ny - 2)
        for copy in copies(0, chunk, orb):
            copy.start()
            flights.append(copy)
    loads[CHUNKS].wait()
    diag = [(pot[x] - 1.75) / 4.5 for x in range(4)]

    for phase in range(2):
        source = (orb, first)[phase]
        for chunk in range(CHUNKS):
            for copy in copies(phase, chunk, source):
                copy.wait_recv()

            @pl.loop(chunk * size, (chunk + 1) * size, unroll=4)
            def _(o):
                tiles = stencil(
                    [source[o, x] for x in range(4)],
                    [xlo[phase, o, x] for x in range(2)],
                    [xhi[phase, o, x] for x in range(2)],
                    ylo[phase, o], yhi[phase, o], diag, row,
                )
                if phase == 0:
                    for x in range(4):
                        first[o, x] = tiles[x]
                    pack(o, tiles, 1)
                else:
                    for x in range(4):
                        filt[pl.ds(pl.multiple_of(o * 32 + 8 * x, 8), 8), :] = 2.0 * tiles[x] - orb[o, x]

            if phase == 0:
                for copy in copies(1, chunk, first):
                    copy.start()
                    flights.append(copy)
            else:
                span = slice(chunk * size, (chunk + 1) * size)
                for r in range(32):
                    flat[span, r * 128:(r + 1) * 128] = filt[
                        pl.ds(chunk * size * 32 + r, size, stride=32), :]
                save = pltpu.make_async_copy(flat.at[span], flat_out.at[span], svs.at[chunk])
                save.start()
                saves.append(save)

    gram = jnp.zeros((3 * width, 3 * width), jnp.float32)
    for step in range(8):
        parts = jnp.concatenate(split3(flat[:, step * 512:(step + 1) * 512]), axis=0)
        gram = gram + lax.dot_general(
            parts, parts, (((1,), (1,)), ((), ())), preferred_element_type=jnp.float32
        )
    total = jnp.zeros((width, 3 * width), jnp.float32)
    for a in (2, 1, 0):
        total = total + gram[a * width:(a + 1) * width]
    total = total[:, 2 * width:] + total[:, width:2 * width] + total[:, :width]
    cells = 4096 * nx * ny
    total = jnp.concatenate([total, jnp.zeros_like(total)], axis=1) / cells
    rows = width // nx
    for i in range(nx):
        gsend[i] = total[i * rows:(i + 1) * rows]

    step1 = []
    for k in range(1, nx):
        to = lax.rem(gx + k, nx)
        copy = pltpu.make_async_remote_copy(
            gsend.at[to], grs.at[k], rss.at[k], rsr.at[k], device_id=(to, gy), device_id_type=MESH)
        copy.start()
        step1.append(copy)
    mine = gsend[gx]
    for k in range(1, nx):
        step1[k - 1].wait_recv()
        mine = mine + grs[k]
    gex[gy] = mine
    step2 = []
    for k in range(1, ny):
        copy = pltpu.make_async_remote_copy(
            gex.at[gy], gex.at[gy], exs.at[k], exr.at[k],
            device_id=(gx, lax.rem(gy + k, ny)), device_id_type=MESH)
        copy.start()
        step2.append(copy)
    for copy in step2:
        copy.wait_recv()
    mine = gex[0]
    for j in range(1, ny):
        mine = mine + gex[j]
    gsum[gx] = mine
    step3 = []
    for k in range(1, nx):
        copy = pltpu.make_async_remote_copy(
            gsum.at[gx], gsum.at[gx], ags.at[k], agr.at[k],
            device_id=(lax.rem(gx + k, nx), gy), device_id_type=MESH)
        copy.start()
        step3.append(copy)
    for copy in step3:
        copy.wait_recv()
    for i in range(nx):
        gram_out[i * rows:(i + 1) * rows, :] = gsum[i]
    for copy in flights + step1 + step2 + step3:
        copy.wait_send()
    for save in saves:
        save.wait()


def solve_kernel(cells, flat_hbm, gram, basis, factor, flat, held, sems):
    load = pltpu.make_async_copy(flat_hbm, flat, sems.at[4])
    load.start()
    width = flat.shape[0]
    groups = width // 8
    lane = lax.broadcasted_iota(jnp.int32, (8, 128), 1)
    row = lax.broadcasted_iota(jnp.int32, (8, 128), 0)
    work = []
    for t in range(groups):
        unit = jnp.where(lane == row + 8 * t + width, 1.0, 0.0)
        work.append(jnp.where(lane < width, gram[8 * t:8 * t + 8, :], unit))
    for p in range(groups):
        spread = [
            [jnp.broadcast_to(work[t][:, 8 * p + k:8 * p + k + 1], (8, 128)) for k in range(8)]
            if t >= p else None
            for t in range(groups)
        ]
        block = [
            [jnp.broadcast_to(spread[p][j][i:i + 1], (8, 128)) for j in range(i + 1)]
            for i in range(8)
        ]
        lines = [jnp.broadcast_to(work[p][k:k + 1], (8, 128)) for k in range(8)]
        roots = []
        for k in range(8):
            inv = 1.0 / block[k][k]
            roots.append(1.0 / jnp.sqrt(block[k][k]))
            scale = [block[i][k] * inv if i > k else None for i in range(8)]
            for i in range(k + 1, 8):
                for j in range(k + 1, i + 1):
                    block[i][j] = block[i][j] - scale[i] * block[j][k]
                lines[i] = lines[i] - scale[i] * lines[k]
            for t in range(p + 1, groups):
                column = spread[t][k]
                for j in range(k + 1, 8):
                    spread[t][j] = spread[t][j] - scale[j] * column
                work[t] = work[t] - (column * inv) * lines[k]
        tile = lines[7] * roots[7]
        for k in range(6, -1, -1):
            tile = jnp.where(row == k, lines[k] * roots[k], tile)
        work[p] = tile
    upper = []
    for t in range(groups):
        upper.append(jnp.where(lane < row + 8 * t, 0.0, work[t]))
    whole = jnp.concatenate(upper, axis=0)
    factor[...] = whole[:, :width]
    inverse = jnp.concatenate(work, axis=0)[:, width:] * (float(cells) ** 0.5)
    a, b, c = split3(inverse)
    lhs = jnp.concatenate([a, b, a, c, b, a], axis=1)
    lines = held.reshape(width * 32, 128)
    stores = []
    load.wait()
    for x in range(4):
        for part in (2 * x, 2 * x + 1):
            y1, y2, y3 = split3(flat[:, part * 512:(part + 1) * 512])
            rhs = jnp.concatenate([y1, y1, y2, y1, y2, y3], axis=0)
            out = jnp.dot(lhs, rhs, preferred_element_type=jnp.float32)
            for i in range(4):
                lines[pl.ds(part * 4 + i, width, stride=32), :] = out[:, i * 128:(i + 1) * 128]
        store = pltpu.make_async_copy(held.at[:, 8 * x:8 * x + 8], basis.at[:, x], sems.at[x])
        store.start()
        stores.append(store)
    for store in stores:
        store.wait()


def shards(mesh, orbitals, potential):
    nx, ny = mesh.shape["gx"], mesh.shape["gy"]
    width = orbitals.shape[0]
    local = orbitals.shape[1] * orbitals.shape[2] * orbitals.shape[3]
    rows = width // nx
    f32 = jnp.float32
    vmem = pl.BlockSpec(memory_space=pltpu.VMEM)
    hbm = pl.BlockSpec(memory_space=pltpu.HBM)
    dma = pltpu.SemaphoreType.DMA
    flat, gram = pl.pallas_call(
        functools.partial(filter_kernel, nx, ny),
        out_shape=[
            jax.ShapeDtypeStruct((width, local), f32),
            jax.ShapeDtypeStruct((width, 128), f32),
        ],
        in_specs=[hbm, hbm],
        out_specs=[hbm, vmem],
        scratch_shapes=[
            pltpu.VMEM(orbitals.shape, f32),
            pltpu.VMEM(potential.shape, f32),
            pltpu.VMEM((width, local), f32),
            pltpu.VMEM(orbitals.shape, f32),
            pltpu.VMEM((width * 32, 128), f32),
            pltpu.VMEM((2, width, 2, 8, 128), f32),
            pltpu.VMEM((2, width, 2, 8, 128), f32),
            pltpu.VMEM((2, width, 8, 128), f32),
            pltpu.VMEM((2, width, 8, 128), f32),
            pltpu.VMEM((2, width, 8, 128), f32),
            pltpu.VMEM((2, width, 8, 128), f32),
            pltpu.VMEM((nx, rows, 128), f32),
            pltpu.VMEM((nx, rows, 128), f32),
            pltpu.VMEM((nx, rows, 128), f32),
            pltpu.VMEM((ny, rows, 128), f32),
            dma((CHUNKS + 1,)), dma((CHUNKS,)),
            dma((2, CHUNKS, 2)), dma((2, CHUNKS, 2)), dma((2, CHUNKS, 2)), dma((2, CHUNKS, 2)),
            dma((nx,)), dma((nx,)), dma((ny,)), dma((ny,)), dma((nx,)), dma((nx,)),
        ],
        compiler_params=pltpu.CompilerParams(
            collective_id=0, has_side_effects=True, vmem_limit_bytes=LIMIT
        ),
        name="filter",
    )(orbitals, potential)
    basis, factor = pl.pallas_call(
        functools.partial(solve_kernel, local * nx * ny),
        out_shape=[
            jax.ShapeDtypeStruct(orbitals.shape, f32),
            jax.ShapeDtypeStruct((width, width), f32),
        ],
        in_specs=[hbm, vmem],
        out_specs=[hbm, vmem],
        scratch_shapes=[pltpu.VMEM((width, local), f32), pltpu.VMEM((width, 32, 128), f32), dma((5,))],
        compiler_params=pltpu.CompilerParams(vmem_limit_bytes=16 << 20),
        name="solve",
    )(flat, gram)
    return basis, factor


def solution(mesh):
    return jax.shard_map(
        functools.partial(shards, mesh),
        mesh=mesh,
        in_specs=(P(None, "gx", "gy", None), P("gx", "gy", None)),
        out_specs=(P(None, "gx", "gy", None), P()),
        check_vma=False,
    )
```
